512 devices in a mesh: owner: 128 (over x, z, core), col: 4 (over y).
Axes of the slice: x: 4, y: 4, z: 16, core: 2. Of those that a mesh axis runs over, the one named last changes fastest.
Arguments:
- embeddings: bfloat16 [131072, 256], P(('owner', 'col')), may hold values from -6 to 6
- adjacency: bfloat16 [131072, 4096], P('owner', 'col'), may hold values from 0 to 0.021972656
- upd_vals: bfloat16 [131072, 256], P(('owner', 'col')), may hold values from 0 to 0.087890625
- upd_dest: int32 [131072, 1], P(('owner', 'col')), may hold values from 0 to 127; in each aligned block of 256 rows (0 to 255, 256 to 511, ...) at most 4 rows name the same one
- upd_target: int32 [131072], P(('owner', 'col')), may hold values from 0 to 4095
- upd_count: int32 [512], P(('owner', 'col')), may hold values from 64 to 256, as said below
- send_row: int32 [262144], P(('owner', 'col')), may hold values from 0 to 255
- send_dest: int32 [262144, 1], P(('owner', 'col')), may hold values from 0 to 127; in each aligned block of 512 rows (0 to 511, 512 to 1023, ...) at most 8 rows name the same one
- affected: int32 [512], P(('owner', 'col')), may hold values 0 or 1
- w_self: bfloat16 [256, 256], replicated, may hold values from -0.375 to 0.375
- w_inter: bfloat16 [256, 256], replicated, may hold values from -0.375 to 0.375
Outputs:
- refreshed: bfloat16 [131072, 256], P(('owner', 'col'))
The draws below stay inside these ranges and needn't reach their ends.
Inputs may be any that keep to these rules, and one draw needn't show every extreme that they name: `upd_dest`: among the update rows of one device at most 4 name the same owner; in some device exactly 4 do. `send_dest`: among the sends of one device at most 8 name the same owner; in some device exactly 8 do. `upd_count`: some device has all 256 update rows live.
All inputs are finite; a program needn't handle non-finite values. No bound on the sum of `affected` on one device may be relied on, other than what follows from the above.
Results may differ from the reference program's by a relative error of at most 0.015.
Values may be sent and summed in bfloat16 or wider, within the bound.
A program may use at most 64 MiB of HBM per device.

```python
import math
import jax
import jax.numpy as jnp
import numpy as np
from jax import lax

D = 256
TILE = 256
RDEV = 256
SEND = 512
UPD = 256
SHARDS = 512
NL = 1024
H = 1024
CAPR = 8
CAPU = 4
TROWS = 4096
ROWS = 131072
N_OWNER = 128
N_COL = 4


def draw_upd_count(key, part):
    key = jax.random.fold_in(key, 7)
    key_low, key_full = jax.random.split(key)
    counts = jax.random.randint(key_low, (SHARDS,), UPD // 4, UPD + 1)
    full_at = jax.random.randint(key_full, (), 0, SHARDS)
    return jnp.where(jnp.arange(SHARDS) == full_at, UPD, counts).astype(jnp.int32)


def set_ends(result, own_key, smallest, top_value):
    spot = [jax.random.randint(jax.random.fold_in(own_key, axis), (), 0, length) for axis, length in enumerate(result.shape)]
    longest = result.shape.index(max(result.shape))
    beside = spot[:longest] + [(spot[longest] + 1) % result.shape[longest]] + spot[longest + 1:]
    return result.at[tuple(spot)].set(smallest).at[tuple(beside)].set(top_value)


def block_scale(key, extent, cuts, low, largest):
    loudness, own = 1.0, jax.random.fold_in(key, 6)
    for axis_at, parts in cuts:
        heights = jnp.exp(jax.random.uniform(jax.random.fold_in(own, axis_at), (parts,), jnp.float32, low / len(cuts), largest / len(cuts)))
        loudness = loudness * jnp.repeat(heights, extent[axis_at] // parts).reshape([-1 if axis == axis_at else 1 for axis in range(len(extent))])
    return loudness


def deal_out(own_key, own, number, rows, number_of, top, reach, lean):
    sequence = jax.random.permutation(own_key, number_of)
    packed, ordinary = portions_of(number_of, rows * top, reach, lean, True), portions_of(number_of, rows * top, reach, lean, False)
    places = jnp.arange(number_of)

    def named(lengths, rotation):
        used = int((lengths > 0).sum())
        fixed = max(1, used // 4)
        moved = fixed + (places - fixed + rotation * (used - fixed)) % max(1, number_of - fixed)
        return jnp.zeros((number_of,), jnp.int32).at[sequence[jnp.where(places < fixed, places, moved)]].set(jnp.asarray(lengths, jnp.int32))

    lengths = jnp.where(number % 4 == 0, named(packed, number // 4), named(ordinary, number - number // 4 - 1))
    mixed = jax.random.permutation(jax.random.fold_in(own, 3), number_of)
    source_of, sink = mixed[0:number_of // 2 * 2:2], mixed[1:number_of // 2 * 2:2]
    slack = jnp.minimum(lengths[source_of] - 1, reach - lengths[sink]) // 2
    slack = jnp.where((source_of == sequence[0]) | (sink == sequence[0]) | (lengths[sink] == 0), 0, jnp.maximum(slack, 0))
    moved = jax.random.randint(jax.random.fold_in(own, 4), (number_of // 2,), 0, 1 << 20) % (slack + 1)
    lengths = lengths.at[source_of].add(-moved).at[sink].add(moved)
    labels = jnp.searchsorted(jnp.cumsum(lengths), jnp.arange(rows * top), side="right").astype(jnp.int32)
    table = labels.reshape(top, rows).T
    table = table[jax.random.permutation(jax.random.fold_in(own, 1), rows)]
    rotation = jax.random.randint(jax.random.fold_in(own, 2), (rows, 1), 0, top)
    return jnp.take_along_axis(table, (jnp.arange(top)[None, :] + rotation) % top, axis=1)


def portions_of(amount, total, most, slope, full):
    weights = [(1 << 20) // math.isqrt(grade ** slope) + 1 for grade in range(1, amount + 1)]
    largest = most if full else min(most, max(-(-total // amount), total * weights[0] // sum(weights)))
    least = 1 if total - largest >= amount - 1 else 0
    given, spare = [largest] + [least] * (amount - 1), total - largest - least * (amount - 1)
    while spare > 0:
        candidates = [i for i in range(1, amount) if given[i] < largest] or [i for i in range(1, amount) if given[i] < most]
        pool, budget = sum([weights[i] for i in candidates]), spare
        for i in candidates:
            more = min(most - given[i], max(1, budget * weights[i] // pool), spare)
            given[i] = given[i] + more
            spare = spare - more
    return np.array(given)


def gaussian(key, extent, deviation, reach, shards=(), kind=jnp.bfloat16):
    array = deviation * jax.random.normal(key, extent, jnp.float32)
    if shards:
        array = array * block_scale(key, extent, shards, -0.22, 0.18)
    return jnp.clip(array, -reach, reach).astype(kind)


def setup_inputs(seed: int = 0) -> dict:
    arg_keys = jax.random.split(jax.random.key(seed), 12)
    embeddings = gaussian(arg_keys[0], (ROWS, D), 1.0, 6.0, ((0, 512),))
    adjacency = jnp.clip(0.021972656 * jax.random.uniform(arg_keys[1], (N_OWNER * NL, N_COL * H), jnp.float32) ** block_scale(arg_keys[1], (N_OWNER * NL, N_COL * H), ((0, 128), (1, 4)), -0.2, 0.2), 0.0, 0.021972656).astype(jnp.bfloat16)
    upd_vals = jnp.clip(0.087890625 * jax.random.uniform(arg_keys[2], (SHARDS * UPD, TILE), jnp.float32) ** block_scale(arg_keys[2], (SHARDS * UPD, TILE), ((0, 512),), -0.2, 0.2), 0.0, 0.087890625).astype(jnp.bfloat16)
    upd_dest_keys = jax.random.split(jax.random.fold_in(arg_keys[3], 1), (SHARDS * UPD) // UPD)
    upd_dest_turns = jax.random.permutation(jax.random.fold_in(arg_keys[3], 3), (SHARDS * UPD) // UPD)
    upd_dest = jax.vmap(lambda own, number: deal_out(jax.random.fold_in(arg_keys[3], 2), own, number, UPD, N_OWNER, 1, CAPU, 2))(upd_dest_keys, upd_dest_turns).reshape((SHARDS * UPD, 1))
    upd_target = set_ends(jax.random.randint(arg_keys[4], (SHARDS * UPD,), 0, TROWS), jax.random.fold_in(arg_keys[4], 1), 0, TROWS - 1).astype(jnp.int32)
    upd_count = draw_upd_count(jax.random.fold_in(arg_keys[11], 71), 0)
    send_row = set_ends(jax.random.randint(arg_keys[6], (SHARDS * SEND,), 0, RDEV), jax.random.fold_in(arg_keys[6], 1), 0, RDEV - 1).astype(jnp.int32)
    send_dest_keys = jax.random.split(jax.random.fold_in(arg_keys[7], 1), (SHARDS * SEND) // SEND)
    send_dest_turns = jax.random.permutation(jax.random.fold_in(arg_keys[7], 3), (SHARDS * SEND) // SEND)
    send_dest = jax.vmap(lambda own, number: deal_out(jax.random.fold_in(arg_keys[7], 2), own, number, SEND, N_OWNER, 1, CAPR, 2))(send_dest_keys, send_dest_turns).reshape((SHARDS * SEND, 1))
    affected = set_ends((jax.random.randint(arg_keys[8], (SHARDS,), 0, 4) < 3).astype(jnp.int32), jax.random.fold_in(arg_keys[8], 1), 0, 1)
    w_self = gaussian(arg_keys[9], (D, D), D ** -0.5, 0.375)
    w_inter = gaussian(arg_keys[10], (D, D), D ** -0.5, 0.375)
    return dict(embeddings=embeddings, adjacency=adjacency, upd_vals=upd_vals, upd_dest=upd_dest, upd_target=upd_target, upd_count=upd_count, send_row=send_row, send_dest=send_dest, affected=affected, w_self=w_self, w_inter=w_inter)


def slot_positions(target_owner, is_live, owners, capacity):
    onehot = jnp.logical_and(target_owner[:, None] == jnp.arange(owners, dtype=jnp.int32)[None, :], is_live[:, None]).astype(jnp.int32)
    running = jnp.cumsum(onehot, axis=0) - 1
    slot_rank = jnp.sum(running * onehot, axis=1)
    return jnp.where(is_live, target_owner * capacity + slot_rank, owners * capacity).astype(jnp.int32)


def reference(embeddings, adjacency, upd_vals, upd_dest, upd_target, upd_count, send_row, send_dest, affected, w_self, w_inter):
    emb_dev = embeddings.reshape(SHARDS, RDEV, D)

    def pack_halo(items):
        rows_dev, row_ids, owner_ids = items
        slots = slot_positions(owner_ids, jnp.ones(owner_ids.shape, jnp.bool_), N_OWNER, CAPR)
        return jnp.zeros((N_OWNER * CAPR, D), jnp.bfloat16).at[slots].set(rows_dev[row_ids], mode="drop")

    sent = lax.map(pack_halo, (emb_dev, send_row.reshape(SHARDS, SEND), send_dest.reshape(SHARDS, SEND)))
    sent = sent.reshape(N_OWNER, N_COL, N_OWNER, CAPR, D)
    halo = jnp.transpose(sent, (2, 1, 0, 3, 4)).reshape(SHARDS, H, D)

    def pack_updates(items):
        values, targets, owner_ids, count = items
        is_live = jnp.arange(UPD, dtype=jnp.int32) < count
        slots = slot_positions(owner_ids, is_live, N_OWNER, CAPU)
        bucket_vals = jnp.zeros((N_OWNER * CAPU, TILE), jnp.bfloat16).at[slots].set(values, mode="drop")
        bucket_targets = jnp.full((N_OWNER * CAPU,), TROWS, jnp.int32).at[slots].set(targets, mode="drop")
        return bucket_vals, bucket_targets

    bucket_vals, bucket_targets = lax.map(pack_updates, (upd_vals.reshape(SHARDS, UPD, TILE), upd_target.reshape(SHARDS, UPD), upd_dest.reshape(SHARDS, UPD), upd_count))
    got_vals = jnp.transpose(bucket_vals.reshape(N_OWNER, N_COL, N_OWNER, CAPU, TILE), (2, 1, 0, 3, 4)).reshape(SHARDS, N_OWNER * CAPU, TILE)
    got_targets = jnp.transpose(bucket_targets.reshape(N_OWNER, N_COL, N_OWNER, CAPU), (2, 1, 0, 3)).reshape(SHARDS, N_OWNER * CAPU)

    def propagate(index):
        owner_at = (index // N_COL).astype(jnp.int32)
        col_at = (index % N_COL).astype(jnp.int32)
        block = lax.dynamic_slice(adjacency, (owner_at * NL, col_at * H), (NL, H))
        delta_sum = jnp.zeros((TROWS, TILE), jnp.float32).at[got_targets[index]].add(got_vals[index].astype(jnp.float32), mode="drop")
        rounded = (block.reshape(TROWS, TILE).astype(jnp.float32) + delta_sum).astype(jnp.bfloat16)
        widened = lax.optimization_barrier(rounded).astype(jnp.float32).reshape(NL, H)
        product = jnp.dot(widened, halo[index].astype(jnp.float32), precision=lax.Precision.HIGHEST)
        return product.astype(jnp.bfloat16)

    partials = lax.map(propagate, jnp.arange(SHARDS, dtype=jnp.int32))
    partials = lax.optimization_barrier(partials).astype(jnp.float32)
    neighbours = jnp.sum(partials.reshape(N_OWNER, N_COL, NL, D), axis=1).reshape(ROWS, D)
    emb_wide = embeddings.astype(jnp.float32)
    self_sum = (neighbours + emb_wide).astype(jnp.bfloat16)
    inter = (neighbours * emb_wide).astype(jnp.bfloat16)
    preact = jnp.dot(self_sum, w_self, preferred_element_type=jnp.float32) + jnp.dot(inter, w_inter, preferred_element_type=jnp.float32)
    layer_out = jnp.where(preact >= 0, preact, 0.2 * preact).astype(jnp.bfloat16)
    row_flags = jnp.repeat(affected, RDEV)[:, None] > 0
    return jnp.where(row_flags, layer_out, embeddings)
```

```python
import functools

import jax
import jax.numpy as jnp
from jax import lax
from jax.experimental import pallas as pl
from jax.experimental.pallas import tpu as pltpu
from jax.sharding import PartitionSpec as P

MESH = pl.DeviceIdType.MESH
BF16, F32, I32 = jnp.bfloat16, jnp.float32, jnp.int32
NX, NZ, NK, NC = 4, 16, 2, 4
NQ = NX * NK
OWNERS = NX * NZ * NK
CAPR, CAPU = 8, 4
D = 256
NL = 1024
ORDER = [8] + [s * d for d in range(7, 0, -1) for s in (1, -1)] + [0]
UGRP, HGRP = 4, 2


def owner_of(x, z, k):
    return (x * NZ + z) * NK + k


def iota(shape, dim):
    return lax.broadcasted_iota(I32, shape, dim)


def dot(a, b):
    return jnp.dot(a, b, preferred_element_type=F32)


def dot_t(a, b):
    return lax.dot_general(a, b, (((1,), (1,)), ((), ())), preferred_element_type=F32)


def ranks(dest, live):
    n = dest.shape[1]
    hot = iota((OWNERS, n), 0) == dest
    if live is not None:
        hot = jnp.logical_and(hot, live)
    hot = jnp.where(hot, 1.0, 0.0)
    before = jnp.where(iota((n, n), 0) < iota((n, n), 1), 1.0, 0.0).astype(BF16)
    running = dot(hot.astype(BF16), before)
    return jnp.sum(running * hot, axis=0, keepdims=True).astype(I32)


def split_owner(dest):
    z = jnp.bitwise_and(jnp.right_shift(dest, 1), NZ - 1)
    q = jnp.right_shift(dest, 5) * NK + jnp.bitwise_and(dest, 1)
    return z, q


def onehot(rows, lane_index):
    return jnp.where(iota((rows, lane_index.shape[1]), 0) == lane_index, 1.0, 0.0).astype(BF16)


def kernel(
    cnt, aff, emb, adj, uval, udst, utgt, srow, sdst, ws, wi,
    out,
    tile, us, uz, ur, ts, tz, tr, hs, hz, hr, halo, tmat, ps, pr, own,
    adj_sem, us_s, ts_s, hs_s, uz_r, tz_r, hz_r, loc,
    ur_s, tr_s, hr_s, ur_r, tr_r, hr_r, loc2, p_s, p_r,
):
    me, c = lax.axis_index("owner"), lax.axis_index("col")
    x, z, k = me // (NZ * NK), lax.rem(me // NK, NZ), lax.rem(me, NK)
    q = x * NK + k

    def zdev(step, sign):
        return (owner_of(x, lax.rem(z + sign * ORDER[step] + NZ, NZ), k), c)

    def qdev(i):
        return lax.rem(x + i // NK, NX), lax.rem(k + i % NK, NK)

    adj_copy = pltpu.make_async_copy(adj, tile, adj_sem)
    adj_copy.start()

    barrier = pltpu.get_barrier_semaphore()
    greeted = [zdev(s, 1) for s in range(NZ - 1)]
    for i in range(1, NQ):
        xx, kk = qdev(i)
        greeted.append((owner_of(xx, z, kk), c))
    greeted += [(me, lax.rem(c + i, NC)) for i in range(1, NC)]
    for dev in greeted:
        pl.semaphore_signal(barrier, inc=1, device_id=dev, device_id_type=MESH)

    dest = udst[...]
    live = iota(dest.shape, 1) < cnt[0]
    rank = ranks(dest, live)
    zz, qq = split_owner(dest)
    slot = jnp.where(live, zz * (NQ * 8) + qq * 8 + rank, -8)
    slot2 = jnp.concatenate([slot, slot + CAPU], axis=1)
    vals = uval[...]
    stacked = jnp.concatenate([vals[:, :128], vals[:, 128:]], axis=0)
    us[...] = dot(onehot(NZ * NQ * 8, slot2), stacked).astype(BF16).reshape(NZ, NQ, 8, 128)
    tgt = utgt[...] + 1
    row_z = jnp.where(jnp.logical_and(iota((NZ, dest.shape[1]), 0) == zz, live), 1.0, 0.0)
    lane_q = onehot(128, qq * CAPU + rank)
    hi = (row_z * jnp.right_shift(tgt, 6).astype(F32)).astype(BF16)
    lo = (row_z * jnp.bitwise_and(tgt, 63).astype(F32)).astype(BF16)
    sent_targets = (dot_t(hi, lane_q) * 64.0 + dot_t(lo, lane_q)).astype(I32)
    for i in range(NZ):
        ts[i] = sent_targets[i : i + 1]

    pl.semaphore_wait(barrier, len(greeted))

    def zcopy(src, dst, send, recv, step):
        dev = zdev(step, 1)
        return pltpu.make_async_remote_copy(
            src.at[lax.rem(z + ORDER[step] + NZ, NZ)], dst.at[step], send, recv.at[step],
            device_id=dev, device_id_type=MESH,
        )

    ucopies = [zcopy(us, uz, us_s, uz_r, s) for s in range(NZ - 1)]
    tcopies = [zcopy(ts, tz, ts_s, tz_r, s) for s in range(NZ - 1)]
    for s in range(NZ - 1):
        tcopies[s].start()
        ucopies[s].start()
    locals_ = [
        pltpu.make_async_copy(us.at[z], uz.at[NZ - 1], loc.at[0]),
        pltpu.make_async_copy(ts.at[z], tz.at[NZ - 1], loc.at[1]),
    ]
    for copy in locals_:
        copy.start()

    dest = sdst[...]
    rank = ranks(dest, None)
    zz, qq = split_owner(dest)
    place = onehot(OWNERS * CAPR, zz * (NQ * CAPR) + qq * CAPR + rank)
    pick = dot_t(place, onehot(D, srow[...])).astype(BF16)
    rows = dot(pick, emb[...]).reshape(OWNERS, CAPR, D)
    hs[...] = (
        jnp.concatenate([rows[:, :, :128], rows[:, :, 128:]], axis=1)
        .astype(BF16)
        .reshape(NZ, NQ, 2 * CAPR, 128)
    )
    hcopies = [zcopy(hs, hz, hs_s, hz_r, s) for s in range(NZ - 1)]
    for s in range(NZ - 1):
        hcopies[s].start()
    locals_.append(pltpu.make_async_copy(hs.at[z], hz.at[NZ - 1], loc.at[2]))
    locals_[2].start()

    def forward(src, dst, send, recv, grp, g, copies, local):
        steps = pl.ds(g, grp)
        for s in range(g, g + grp):
            if s < NZ - 1:
                copies[s].wait_recv()
            else:
                local.wait()
        for i in (3, 5, 2, 4, 6, 7, 1):
            xx, kk = qdev(i)
            pltpu.make_async_remote_copy(
                src.at[steps, xx * NK + kk], dst.at[q, steps], send, recv.at[g // grp],
                device_id=(owner_of(xx, z, kk), c), device_id_type=MESH,
            ).start()

    for s in range(NZ - 1):
        tcopies[s].wait_recv()
    locals_[1].wait()
    for i in range(1, NQ):
        xx, kk = qdev(i)
        pltpu.make_async_remote_copy(
            tz, tr.at[q], tr_s, tr_r, device_id=(owner_of(xx, z, kk), c), device_id_type=MESH
        ).start()
    own_t = pltpu.make_async_copy(tz, tr.at[q], loc2.at[0])
    own_t.start()
    for g in range(0, NZ, UGRP):
        forward(uz, ur, ur_s, ur_r, UGRP, g, ucopies, locals_[0])
    own_u = pltpu.make_async_copy(uz.at[:, q], ur.at[q], loc2.at[1])
    own_u.start()

    own_t.wait()
    some = tr.at[pl.ds(0, NQ - 1)]
    pltpu.make_async_copy(some, some, tr_r).wait()
    pltpu.make_async_copy(some, some, tr_s).wait()
    own_u.wait()
    for g in range(NZ // UGRP):
        some = ur.at[pl.ds(0, NQ - 1), pl.ds(g * UGRP, UGRP)]
        pltpu.make_async_copy(some, some, ur_r.at[g]).wait()
    some = ur.at[pl.ds(0, NQ - 1)]
    pltpu.make_async_copy(some, some, ur_s).wait()

    for i in range(OWNERS):
        tmat[i : i + 1] = tr[i // NZ, i % NZ]
    got = tmat[...].astype(F32)
    eye = iota((128, 128), 0) == iota((128, 128), 1)
    lanes = []
    for s in range(CAPU):
        column = jnp.sum(jnp.where(iota((128, 128), 1) == q * CAPU + s, got, 0.0), axis=1, keepdims=True)
        lanes.append(jnp.sum(jnp.where(eye, column, 0.0), axis=0, keepdims=True))
    target = jnp.concatenate(lanes, axis=1).astype(I32) - 1
    packed = ur[...].reshape(OWNERS * 8, 128)
    u_row = iota((OWNERS * CAPU, OWNERS * 8), 0)
    u_from = jnp.bitwise_and(u_row, 127) * 8 + jnp.right_shift(u_row, 7)
    m_col = iota((OWNERS * CAPU, OWNERS * 8), 1)
    halves = [
        dot(jnp.where(m_col == u_from + h * CAPU, 1.0, 0.0).astype(BF16), packed) for h in (0, 1)
    ]
    values = jnp.concatenate(halves, axis=1).astype(BF16)

    adj_copy.wait()
    for j in range(4):
        row_of = jnp.where(jnp.bitwise_and(target, 3) == j, jnp.right_shift(target, 2), -1)
        row_of = jnp.where(target < 0, -1, row_of)

        @pl.loop(0, NL // 256)
        def _(b, j=j, row_of=row_of):
            at = (pl.ds(pl.multiple_of(b * 256, 256), 256), pl.ds(j * 256, 256))
            delta = dot(onehot(256, row_of - b * 256), values)
            tile[at] = (tile[at].astype(F32) + delta).astype(BF16)

    for g in range(0, NZ, HGRP):
        forward(hz, hr, hr_s, hr_r, HGRP, g, hcopies, locals_[2])
    own_h = pltpu.make_async_copy(hz.at[:, q], hr.at[q], loc2.at[2])
    own_h.start()
    own_h.wait()
    for g in range(NZ // HGRP):
        some = hr.at[pl.ds(0, NQ - 1), pl.ds(g * HGRP, HGRP)]
        pltpu.make_async_copy(some, some, hr_r.at[g]).wait()
        for s in range(g * HGRP, (g + 1) * HGRP):
            zs = lax.rem(z - ORDER[s] + NZ, NZ)
            for xs in range(NX):
                a = hr[xs * NK, s].astype(F32)
                b = hr[xs * NK + 1, s].astype(F32)
                at = pl.ds(pl.multiple_of((xs * NZ + zs) * 16, 16), 16)
                halo[at, 0:128] = jnp.concatenate([a[:8], b[:8]], axis=0).astype(BF16)
                halo[at, 128:256] = jnp.concatenate([a[8:], b[8:]], axis=0).astype(BF16)

    for i in (2, 1, 3, 0):
        cc = lax.rem(c + i, NC)
        block = tile[pl.ds(pl.multiple_of(cc * 256, 256), 256), :]
        share = dot(block, halo[...]).astype(BF16)
        if i == 0:
            own[...] = share
        else:
            ps[i - 1] = share
            pltpu.make_async_remote_copy(
                ps.at[i - 1], pr.at[i - 1], p_s, p_r, device_id=(me, cc), device_id_type=MESH
            ).start()

    some = hr.at[pl.ds(0, NQ - 1)]
    pltpu.make_async_copy(some, some, hr_s).wait()
    for src, sem in ((us, us_s), (ts, ts_s), (hs, hs_s)):
        some = src.at[pl.ds(0, NZ - 1)]
        pltpu.make_async_copy(some, some, sem).wait()
    pltpu.make_async_copy(pr, pr, p_r).wait()

    neighbours = own[...].astype(F32)
    for i in range(NC - 1):
        neighbours = neighbours + pr[i].astype(F32)
    wide = emb[...].astype(F32)
    self_sum = (neighbours + wide).astype(BF16)
    inter = (neighbours * wide).astype(BF16)
    preact = dot(self_sum, ws[...]) + dot(inter, wi[...])
    layer = jnp.where(preact >= 0, preact, 0.2 * preact)
    out[...] = jnp.where(aff[0] > 0, layer, wide).astype(BF16)
    pltpu.make_async_copy(ps, ps, p_s).wait()


def per_device(
    embeddings, adjacency, upd_vals, upd_dest, upd_target, upd_count,
    send_row, send_dest, affected, w_self, w_inter,
):
    v = pl.BlockSpec(memory_space=pltpu.VMEM)
    s = pl.BlockSpec(memory_space=pltpu.SMEM)
    a = pl.BlockSpec(memory_space=pl.ANY)
    vm = pltpu.VMEM
    dma = pltpu.SemaphoreType.DMA
    u, r = upd_dest.shape[0], send_dest.shape[0]
    return pl.pallas_call(
        kernel,
        out_shape=jax.ShapeDtypeStruct((D, D), BF16),
        in_specs=[s, s, v, a, v, v, v, v, v, v, v],
        out_specs=v,
        scratch_shapes=[
            vm((NL, NL), BF16),
            vm((NZ, NQ, 8, 128), BF16),
            vm((NZ, NQ, 8, 128), BF16),
            vm((NQ, NZ, 8, 128), BF16),
            vm((NZ, 1, 128), I32),
            vm((NZ, 1, 128), I32),
            vm((NQ, NZ, 1, 128), I32),
            vm((NZ, NQ, 16, 128), BF16),
            vm((NZ, NQ, 16, 128), BF16),
            vm((NQ, NZ, 16, 128), BF16),
            vm((OWNERS * CAPR, D), BF16),
            vm((128, 128), I32),
            vm((NC - 1, 256, 256), BF16),
            vm((NC - 1, 256, 256), BF16),
            vm((256, 256), BF16),
            dma, dma, dma, dma, dma((NZ,)), dma((NZ,)), dma((NZ,)), dma((3,)),
            dma, dma, dma, dma((NZ // UGRP,)), dma, dma((NZ // HGRP,)), dma((3,)), dma, dma,
        ],
        compiler_params=pltpu.CompilerParams(
            collective_id=0, has_side_effects=True, vmem_limit_bytes=48 * 2**20
        ),
    )(
        upd_count, affected, embeddings, adjacency, upd_vals,
        upd_dest.reshape(1, u), upd_target.reshape(1, u),
        send_row.reshape(1, r), send_dest.reshape(1, r), w_self, w_inter,
    )


def solution(mesh):
    rows = P(("owner", "col"))
    wide = P(("owner", "col"), None)
    return jax.shard_map(
        per_device,
        mesh=mesh,
        in_specs=(wide, P("owner", "col"), wide, wide, rows, rows, rows, wide, rows, P(), P()),
        out_specs=wide,
        check_vma=False,
    )
```

```python
import functools

import jax
import jax.numpy as jnp
from jax import lax
from jax.experimental import pallas as pl
from jax.experimental.pallas import tpu as pltpu
from jax.sharding import PartitionSpec as P

MESH = pl.DeviceIdType.MESH
BF16, F32, I32 = jnp.bfloat16, jnp.float32, jnp.int32
NX, NZ, NK, NC = 4, 16, 2, 4
NQ = NX * NK
OWNERS = NX * NZ * NK
CAPR, CAPU = 8, 4
D = 256
NL = 1024
ORDER = [8] + [s * d for d in range(7, 0, -1) for s in (1, -1)] + [0]
UGRP, HGRP = 4, 4
RAT = 3
HALF = D // 2

def owner_of(x, z, k):
    return (x * NZ + z) * NK + k


def iota(shape, dim):
    return lax.broadcasted_iota(I32, shape, dim)


def dot(a, b):
    return jnp.dot(a, b, preferred_element_type=F32)


def dot_t(a, b):
    return lax.dot_general(a, b, (((1,), (1,)), ((), ())), preferred_element_type=F32)


def ranks(dest, live):
    n = dest.shape[1]
    hot = iota((OWNERS, n), 0) == dest
    if live is not None:
        hot = jnp.logical_and(hot, live)
    hot = jnp.where(hot, 1.0, 0.0)
    before = jnp.where(iota((n, n), 0) < iota((n, n), 1), 1.0, 0.0).astype(BF16)
    running = dot(hot.astype(BF16), before)
    return jnp.sum(running * hot, axis=0, keepdims=True).astype(I32)


def split_owner(dest):
    z = jnp.bitwise_and(jnp.right_shift(dest, 1), NZ - 1)
    q = jnp.right_shift(dest, 5) * NK + jnp.bitwise_and(dest, 1)
    return z, q


def onehot(rows, lane_index):
    return jnp.where(iota((rows, lane_index.shape[1]), 0) == lane_index, 1.0, 0.0).astype(BF16)


def kernel(
    cnt_h, aff_h, ints_h, emb_h, adj, uval_h, ws_h, wi_h,
    out,
    cnt, aff, ints, emb, uval, ws, wi, in_sem,
    tile, us, uz, ur, ts, tz, tr, hs, hz, hr, halo, tmat, ps, pr, own,
    adj_sem, us_s, ts_s, hs_s, uz_r, tz_r, hz_r, loc,
    ur_s, tr_s, hr_s, ur_r, tr_r, hr_r, loc2, p_s, p_r,
):
    me, c = lax.axis_index("owner"), lax.axis_index("col")
    x, z, k = me // (NZ * NK), lax.rem(me // NK, NZ), lax.rem(me, NK)
    q = x * NK + k

    def zdev(step, sign):
        return (owner_of(x, lax.rem(z + sign * ORDER[step] + NZ, NZ), k), c)

    def qdev(i):
        return lax.rem(x + i // NK, NX), lax.rem(k + i % NK, NK)

    adj_copy = pltpu.make_async_copy(adj, tile, adj_sem)
    inputs = [
        pltpu.make_async_copy(src, dst, in_sem.at[i])
        for i, (src, dst) in enumerate(
            (
                (ints_h, ints), (uval_h, uval), (cnt_h, cnt), (aff_h, aff), (emb_h, emb), (ws_h, ws), (wi_h, wi),
            )
        )
    ]
    for copy in inputs:
        copy.start()
    adj_copy.start()

    barrier = pltpu.get_barrier_semaphore()
    greeted = [zdev(s, 1) for s in range(NZ - 1)]
    for i in range(1, NQ):
        xx, kk = qdev(i)
        greeted.append((owner_of(xx, z, kk), c))
    greeted += [(me, lax.rem(c + i, NC)) for i in range(1, NC)]
    for dev in greeted:
        pl.semaphore_signal(barrier, inc=1, device_id=dev, device_id_type=MESH)

    for copy in inputs[:3]:
        copy.wait()
    udst, utgt = ints[:, 0:256], ints[:, 256:512]
    srow, sdst = ints[:, 512:1024], ints[:, 1024:1536]
    dest = udst
    live = iota(dest.shape, 1) < cnt[0]
    rank = ranks(dest, live)
    zz, qq = split_owner(dest)
    slot = jnp.where(live, zz * (NQ * 8) + qq * 8 + rank, -8)
    slot2 = jnp.concatenate([slot, slot + CAPU], axis=1)
    vals = uval[...]
    stacked = jnp.concatenate([vals[:, :128], vals[:, 128:]], axis=0)
    us[...] = dot(onehot(NZ * NQ * 8, slot2), stacked).astype(BF16).reshape(NZ, NQ, 8, 128)
    tgt = utgt + 1
    row_z = jnp.where(jnp.logical_and(iota((NZ, dest.shape[1]), 0) == zz, live), 1.0, 0.0)
    lane_q = onehot(128, qq * CAPU + rank)
    hi = (row_z * jnp.right_shift(tgt, 6).astype(F32)).astype(BF16)
    lo = (row_z * jnp.bitwise_and(tgt, 63).astype(F32)).astype(BF16)
    sent_targets = (dot_t(hi, lane_q) * 64.0 + dot_t(lo, lane_q)).astype(I32)
    for i in range(NZ):
        ts[i] = sent_targets[i : i + 1]

    pl.semaphore_wait(barrier, len(greeted))

    def zcopy(src, dst, send, recv, step):
        dev = zdev(step, 1)
        return pltpu.make_async_remote_copy(
            src.at[lax.rem(z + ORDER[step] + NZ, NZ)], dst.at[step], send, recv.at[step],
            device_id=dev, device_id_type=MESH,
        )

    ucopies = [zcopy(us, uz, us_s, uz_r, s) for s in range(NZ - 1)]
    tcopies = [zcopy(ts, tz, ts_s, tz_r, s) for s in range(NZ - 1)]
    for s in range(NZ - 1):
        tcopies[s].start()
        ucopies[s].start()
    locals_ = [
        pltpu.make_async_copy(us.at[z], uz.at[NZ - 1], loc.at[0]),
        pltpu.make_async_copy(ts.at[z], tz.at[NZ - 1], loc.at[1]),
    ]
    for copy in locals_:
        copy.start()

    for copy in inputs[3:]:
        copy.wait()
    dest = sdst
    rank = ranks(dest, None)
    zz, qq = split_owner(dest)
    place = onehot(OWNERS * CAPR, zz * (NQ * CAPR) + qq * CAPR + rank)
    pick = dot_t(place, onehot(D, srow)).astype(BF16)
    rows = dot(pick, emb[...]).astype(BF16)
    for h in (0, 1):
        hs[h] = rows[:, h * HALF : (h + 1) * HALF].reshape(NZ, NQ, CAPR, HALF)
    hcopies = [
        [zcopy(hs.at[h], hz.at[h], hs_s.at[h], hz_r.at[h], s) for s in range(NZ - 1)] for h in (0, 1)
    ]
    for h in (0, 1):
        locals_.append(pltpu.make_async_copy(hs.at[h, z], hz.at[h, NZ - 1], loc.at[2 + h]))
        locals_[2 + h].start()

    def send_half(h):
        for s in range(NZ - 1):
            hcopies[h][s].start()

    send_half(0)

    def forward(src, dst, send, recv, grp, g, copies, local):
        steps = pl.ds(g, grp)
        for s in range(g, g + grp):
            if s < NZ - 1:
                copies[s].wait_recv()
            else:
                local.wait()
        for i in (3, 5, 2, 4, 6, 7, 1):
            xx, kk = qdev(i)
            pltpu.make_async_remote_copy(
                src.at[steps, xx * NK + kk], dst.at[q, steps], send, recv.at[g // grp],
                device_id=(owner_of(xx, z, kk), c), device_id_type=MESH,
            ).start()

    for s in range(NZ - 1):
        tcopies[s].wait_recv()
    locals_[1].wait()
    for i in range(1, NQ):
        xx, kk = qdev(i)
        pltpu.make_async_remote_copy(
            tz, tr.at[q], tr_s, tr_r, device_id=(owner_of(xx, z, kk), c), device_id_type=MESH
        ).start()
    own_t = pltpu.make_async_copy(tz, tr.at[q], loc2.at[0])
    own_t.start()
    for g in range(0, NZ, UGRP):
        forward(uz, ur, ur_s, ur_r, UGRP, g, ucopies, locals_[0])
        if g == RAT * UGRP:
            send_half(1)
    own_u = pltpu.make_async_copy(uz.at[:, q], ur.at[q], loc2.at[1])
    own_u.start()

    own_t.wait()
    some = tr.at[pl.ds(0, NQ - 1)]
    pltpu.make_async_copy(some, some, tr_r).wait()
    pltpu.make_async_copy(some, some, tr_s).wait()
    own_u.wait()
    for g in range(NZ // UGRP):
        some = ur.at[pl.ds(0, NQ - 1), pl.ds(g * UGRP, UGRP)]
        pltpu.make_async_copy(some, some, ur_r.at[g]).wait()
    some = ur.at[pl.ds(0, NQ - 1)]
    pltpu.make_async_copy(some, some, ur_s).wait()

    for i in range(OWNERS):
        tmat[i : i + 1] = tr[i // NZ, i % NZ]
    got = tmat[...].astype(F32)
    eye = iota((128, 128), 0) == iota((128, 128), 1)
    lanes = []
    for s in range(CAPU):
        column = jnp.sum(jnp.where(iota((128, 128), 1) == q * CAPU + s, got, 0.0), axis=1, keepdims=True)
        lanes.append(jnp.sum(jnp.where(eye, column, 0.0), axis=0, keepdims=True))
    target = jnp.concatenate(lanes, axis=1).astype(I32) - 1
    packed = ur[...].reshape(OWNERS * 8, 128)
    u_row = iota((OWNERS * CAPU, OWNERS * 8), 0)
    u_from = jnp.bitwise_and(u_row, 127) * 8 + jnp.right_shift(u_row, 7)
    m_col = iota((OWNERS * CAPU, OWNERS * 8), 1)
    halves = [
        dot(jnp.where(m_col == u_from + h * CAPU, 1.0, 0.0).astype(BF16), packed) for h in (0, 1)
    ]
    values = jnp.concatenate(halves, axis=1).astype(BF16)

    adj_copy.wait()
    for j in range(4):
        row_of = jnp.where(jnp.bitwise_and(target, 3) == j, jnp.right_shift(target, 2), -1)
        row_of = jnp.where(target < 0, -1, row_of)

        @pl.loop(0, NL // 256)
        def _(b, j=j, row_of=row_of):
            at = (pl.ds(pl.multiple_of(b * 256, 256), 256), pl.ds(j * 256, 256))
            delta = dot(onehot(256, row_of - b * 256), values)
            tile[at] = (tile[at].astype(F32) + delta).astype(BF16)

    def half_product(h):
        for g in range(0, NZ, HGRP):
            forward(
                hz.at[h], hr.at[h], hr_s.at[h], hr_r.at[h], HGRP, g, hcopies[h], locals_[2 + h]
            )
        own_h = pltpu.make_async_copy(hz.at[h, :, q], hr.at[h, q], loc2.at[2 + h])
        own_h.start()
        own_h.wait()
        for g in range(NZ // HGRP):
            some = hr.at[h, pl.ds(0, NQ - 1), pl.ds(g * HGRP, HGRP)]
            pltpu.make_async_copy(some, some, hr_r.at[h, g]).wait()
            for s in range(g * HGRP, (g + 1) * HGRP):
                zs = lax.rem(z - ORDER[s] + NZ, NZ)
                for xs in range(NX):
                    pair = [hr[h, xs * NK + kk, s].astype(F32) for kk in range(NK)]
                    at = pl.ds(pl.multiple_of((xs * NZ + zs) * 16, 16), 16)
                    halo[h, at, :] = jnp.concatenate(pair, axis=0).astype(BF16)
        for i in (2, 1, 3, 0):
            cc = lax.rem(c + i, NC)
            block = tile[pl.ds(pl.multiple_of(cc * 256, 256), 256), :]
            share = dot(block, halo[h]).astype(BF16)
            if i == 0:
                own[h] = share
            else:
                ps[h, i - 1] = share
                pltpu.make_async_remote_copy(
                    ps.at[h, i - 1], pr.at[h, i - 1], p_s.at[h], p_r.at[h],
                    device_id=(me, cc), device_id_type=MESH,
                ).start()

    half_product(0)
    half_product(1)

    preact = jnp.zeros((256, D), F32)
    for h in (0, 1):
        pltpu.make_async_copy(pr.at[h], pr.at[h], p_r.at[h]).wait()
        neighbours = own[h].astype(F32)
        for i in range(NC - 1):
            neighbours = neighbours + pr[h, i].astype(F32)
        at = pl.ds(h * HALF, HALF)
        wide = emb[:, at].astype(F32)
        self_sum = (neighbours + wide).astype(BF16)
        inter = (neighbours * wide).astype(BF16)
        preact = preact + dot(self_sum, ws[at, :]) + dot(inter, wi[at, :])
    layer = jnp.where(preact >= 0, preact, 0.2 * preact)
    out[...] = jnp.where(aff[0] > 0, layer, emb[...].astype(F32)).astype(BF16)

    for h in (0, 1):
        some = hr.at[h, pl.ds(0, NQ - 1)]
        pltpu.make_async_copy(some, some, hr_s.at[h]).wait()
        some = hs.at[h, pl.ds(0, NZ - 1)]
        pltpu.make_async_copy(some, some, hs_s.at[h]).wait()
        pltpu.make_async_copy(ps.at[h], ps.at[h], p_s.at[h]).wait()
    for src, sem in ((us, us_s), (ts, ts_s)):
        some = src.at[pl.ds(0, NZ - 1)]
        pltpu.make_async_copy(some, some, sem).wait()


def per_device(
    embeddings, adjacency, upd_vals, upd_dest, upd_target, upd_count,
    send_row, send_dest, affected, w_self, w_inter,
):
    v = pl.BlockSpec(memory_space=pltpu.VMEM)
    a = pl.BlockSpec(memory_space=pltpu.HBM)
    vm = pltpu.VMEM
    dma = pltpu.SemaphoreType.DMA
    u, r = upd_dest.shape[0], send_dest.shape[0]
    ints = jnp.concatenate(
        [
            upd_dest.reshape(1, u), upd_target.reshape(1, u), send_row.reshape(1, r),
            send_dest.reshape(1, r),
        ],
        axis=1,
    )
    return pl.pallas_call(
        kernel,
        out_shape=jax.ShapeDtypeStruct((D, D), BF16),
        in_specs=[a] * 8,
        out_specs=v,
        scratch_shapes=[
            pltpu.SMEM((1,), I32), pltpu.SMEM((1,), I32), vm((1, 1536), I32), vm((D, D), BF16), vm((u, D), BF16), vm((D, D), BF16), vm((D, D), BF16),
            dma((7,)),
            vm((NL, NL), BF16),
            vm((NZ, NQ, 8, 128), BF16),
            vm((NZ, NQ, 8, 128), BF16),
            vm((NQ, NZ, 8, 128), BF16),
            vm((NZ, 1, 128), I32),
            vm((NZ, 1, 128), I32),
            vm((NQ, NZ, 1, 128), I32),
            vm((2, NZ, NQ, CAPR, HALF), BF16),
            vm((2, NZ, NQ, CAPR, HALF), BF16),
            vm((2, NQ, NZ, CAPR, HALF), BF16),
            vm((2, OWNERS * CAPR, HALF), BF16),
            vm((128, 128), I32),
            vm((2, NC - 1, 256, HALF), BF16),
            vm((2, NC - 1, 256, HALF), BF16),
            vm((2, 256, HALF), BF16),
            dma, dma, dma, dma((2,)), dma((NZ,)), dma((NZ,)), dma((2, NZ)), dma((4,)),
            dma, dma, dma((2,)), dma((NZ // UGRP,)), dma, dma((2, NZ // HGRP)), dma((4,)),
            dma((2,)), dma((2,)),
        ],
        compiler_params=pltpu.CompilerParams(
            collective_id=0, has_side_effects=True, vmem_limit_bytes=3440 * 2**14
        ),
    )(upd_count, affected, ints, embeddings, adjacency, upd_vals, w_self, w_inter)


def solution(mesh):
    rows = P(("owner", "col"))
    wide = P(("owner", "col"), None)
    return jax.shard_map(
        per_device,
        mesh=mesh,
        in_specs=(wide, P("owner", "col"), wide, wide, rows, rows, rows, wide, rows, P(), P()),
        out_specs=wide,
        check_vma=False,
    )
```

```python
import functools

import jax
import jax.numpy as jnp
from jax import lax
from jax.experimental import pallas as pl
from jax.experimental.pallas import tpu as pltpu
from jax.sharding import PartitionSpec as P

MESH = pl.DeviceIdType.MESH
BF16, F32, I32 = jnp.bfloat16, jnp.float32, jnp.int32
NX, NZ, NK, NC = 4, 16, 2, 4
NQ = NX * NK
OWNERS = NX * NZ * NK
CAPR, CAPU = 8, 4
D = 256
NL = 1024
ORDER = [8] + [s * d for d in range(7, 0, -1) for s in (1, -1)] + [0]
GROUPS = [range(0, 4), range(4, 8), range(8, 12), range(12, 15), range(15, 16)]
HALF = D // 2

def owner_of(x, z, k):
    return (x * NZ + z) * NK + k


def iota(shape, dim):
    return lax.broadcasted_iota(I32, shape, dim)


def dot(a, b):
    return jnp.dot(a, b, preferred_element_type=F32)


def dot_t(a, b):
    return lax.dot_general(a, b, (((1,), (1,)), ((), ())), preferred_element_type=F32)


def ranks(dest, live):
    n = dest.shape[1]
    hot = iota((OWNERS, n), 0) == dest
    if live is not None:
        hot = jnp.logical_and(hot, live)
    hot = jnp.where(hot, 1.0, 0.0)
    before = jnp.where(iota((n, n), 0) < iota((n, n), 1), 1.0, 0.0).astype(BF16)
    running = dot(hot.astype(BF16), before)
    return jnp.sum(running * hot, axis=0, keepdims=True).astype(I32)


def split_owner(dest):
    z = jnp.bitwise_and(jnp.right_shift(dest, 1), NZ - 1)
    q = jnp.right_shift(dest, 5) * NK + jnp.bitwise_and(dest, 1)
    return z, q


def onehot(rows, lane_index):
    return jnp.where(iota((rows, lane_index.shape[1]), 0) == lane_index, 1.0, 0.0).astype(BF16)


def kernel(
    cnt_h, aff_h, ints_h, emb_h, adj, uval_h, ws_h, wi_h,
    out,
    cnt, aff, ints, emb, uval, ws, wi, in_sem,
    tile, us, ur, ts, tz, tr, hs, hr, halo, tmat, ps, pr, own,
    adj_sem, us_s, ts_s, hs_s, tz_r, loc,
    tr_s, ur_r, tr_r, hr_r, own_t_s, p_s, p_r,
):
    me, c = lax.axis_index("owner"), lax.axis_index("col")
    x, z, k = me // (NZ * NK), lax.rem(me // NK, NZ), lax.rem(me, NK)
    q = x * NK + k

    def zdev(step, sign):
        return (owner_of(x, lax.rem(z + sign * ORDER[step] + NZ, NZ), k), c)

    def qdev(i):
        return lax.rem(x + i // NK, NX), lax.rem(k + i % NK, NK)

    adj_copy = pltpu.make_async_copy(adj, tile, adj_sem)
    inputs = [
        pltpu.make_async_copy(src, dst, in_sem.at[i])
        for i, (src, dst) in enumerate(
            (
                (ints_h, ints), (uval_h, uval), (cnt_h, cnt), (aff_h, aff), (emb_h, emb), (ws_h, ws), (wi_h, wi),
            )
        )
    ]
    for copy in inputs:
        copy.start()
    adj_copy.start()

    barrier = pltpu.get_barrier_semaphore()
    greeted = []
    for s in range(NZ):
        for i in range(NQ):
            if s < NZ - 1 or i:
                xx, kk = qdev(i)
                greeted.append((owner_of(xx, lax.rem(z + ORDER[s] + NZ, NZ), kk), c))
    greeted += [(me, lax.rem(c + i, NC)) for i in range(1, NC)]
    for dev in greeted:
        pl.semaphore_signal(barrier, inc=1, device_id=dev, device_id_type=MESH)

    for copy in inputs[:3]:
        copy.wait()
    udst, utgt = ints[:, 0:256], ints[:, 256:512]
    srow, sdst = ints[:, 512:1024], ints[:, 1024:1536]
    dest = udst
    live = iota(dest.shape, 1) < cnt[0]
    rank = ranks(dest, live)
    zz, qq = split_owner(dest)
    slot = jnp.where(live, zz * (NQ * 8) + qq * 8 + rank, -8)
    slot2 = jnp.concatenate([slot, slot + CAPU], axis=1)
    vals = uval[...]
    stacked = jnp.concatenate([vals[:, :128], vals[:, 128:]], axis=0)
    us[...] = dot(onehot(NZ * NQ * 8, slot2), stacked).astype(BF16).reshape(NZ, NQ, 8, 128)
    tgt = utgt + 1
    row_z = jnp.where(jnp.logical_and(iota((NZ, dest.shape[1]), 0) == zz, live), 1.0, 0.0)
    lane_q = onehot(128, qq * CAPU + rank)
    hi = (row_z * jnp.right_shift(tgt, 6).astype(F32)).astype(BF16)
    lo = (row_z * jnp.bitwise_and(tgt, 63).astype(F32)).astype(BF16)
    sent_targets = (dot_t(hi, lane_q) * 64.0 + dot_t(lo, lane_q)).astype(I32)
    for i in range(NZ):
        ts[i] = sent_targets[i : i + 1]

    pl.semaphore_wait(barrier, len(greeted))

    def zcopy(src, dst, send, recv, step):
        dev = zdev(step, 1)
        return pltpu.make_async_remote_copy(
            src.at[lax.rem(z + ORDER[step] + NZ, NZ)], dst.at[step], send, recv.at[step],
            device_id=dev, device_id_type=MESH,
        )

    def direct(src, dst, send, recv):
        for i in (3, 5, 2, 4, 6, 7, 1, 0):
            for s in range(NZ):
                zz = lax.rem(z + ORDER[s] + NZ, NZ)
                g = [g for g, steps in enumerate(GROUPS) if s in steps][0]
                if s < NZ - 1 or i:
                    xx, kk = qdev(i)
                    pltpu.make_async_remote_copy(
                        src.at[zz, xx * NK + kk], dst.at[q, s], send.at[g], recv.at[g],
                        device_id=(owner_of(xx, zz, kk), c), device_id_type=MESH,
                    ).start()

    def wait_group(src, sem, g):
        some = src.at[pl.ds(0, len(GROUPS[g]))]
        if g == len(GROUPS) - 1:
            some = src.at[0, pl.ds(0, NQ - 1)]
        pltpu.make_async_copy(some, some, sem.at[g]).wait()

    tcopies = [zcopy(ts, tz, ts_s, tz_r, s) for s in range(NZ - 1)]
    for s in range(NZ - 1):
        tcopies[s].start()
    direct(us, ur, us_s, ur_r)
    locals_ = [
        pltpu.make_async_copy(us.at[z, q], ur.at[q, NZ - 1], loc.at[0]),
        pltpu.make_async_copy(ts.at[z], tz.at[NZ - 1], loc.at[1]),
    ]
    for copy in locals_:
        copy.start()

    for copy in inputs[3:]:
        copy.wait()
    dest = sdst
    rank = ranks(dest, None)
    zz, qq = split_owner(dest)
    place = onehot(OWNERS * CAPR, zz * (NQ * CAPR) + qq * CAPR + rank)
    pick = dot_t(place, onehot(D, srow)).astype(BF16)
    rows = dot(pick, emb[...]).astype(BF16)
    for h in (0, 1):
        hs[h] = rows[:, h * HALF : (h + 1) * HALF].reshape(NZ, NQ, CAPR, HALF)
    direct(hs.at[0], hr.at[0], hs_s.at[0], hr_r.at[0])
    for h in (0, 1):
        locals_.append(pltpu.make_async_copy(hs.at[h, z, q], hr.at[h, q, NZ - 1], loc.at[2 + h]))
        locals_[2 + h].start()

    for s in range(NZ - 1):
        tcopies[s].wait_recv()
    locals_[1].wait()
    for i in range(1, NQ):
        xx, kk = qdev(i)
        pltpu.make_async_remote_copy(
            tz, tr.at[q], tr_s, tr_r, device_id=(owner_of(xx, z, kk), c), device_id_type=MESH
        ).start()
    own_t = pltpu.make_async_copy(tz, tr.at[q], own_t_s)
    own_t.start()
    direct(hs.at[1], hr.at[1], hs_s.at[1], hr_r.at[1])
    own_t.wait()
    some = tr.at[pl.ds(0, NQ - 1)]
    pltpu.make_async_copy(some, some, tr_r).wait()
    pltpu.make_async_copy(some, some, tr_s).wait()
    locals_[0].wait()
    for g in range(len(GROUPS)):
        wait_group(us, ur_r, g)

    for i in range(OWNERS):
        tmat[i : i + 1] = tr[i // NZ, i % NZ]
    got = tmat[...].astype(F32)
    eye = iota((128, 128), 0) == iota((128, 128), 1)
    lanes = []
    for s in range(CAPU):
        column = jnp.sum(jnp.where(iota((128, 128), 1) == q * CAPU + s, got, 0.0), axis=1, keepdims=True)
        lanes.append(jnp.sum(jnp.where(eye, column, 0.0), axis=0, keepdims=True))
    target = jnp.concatenate(lanes, axis=1).astype(I32) - 1
    packed = ur[...].reshape(OWNERS * 8, 128)
    u_row = iota((OWNERS * CAPU, OWNERS * 8), 0)
    u_from = jnp.bitwise_and(u_row, 127) * 8 + jnp.right_shift(u_row, 7)
    m_col = iota((OWNERS * CAPU, OWNERS * 8), 1)
    halves = [
        dot(jnp.where(m_col == u_from + h * CAPU, 1.0, 0.0).astype(BF16), packed) for h in (0, 1)
    ]
    values = jnp.concatenate(halves, axis=1).astype(BF16)

    adj_copy.wait()
    for j in range(4):
        row_of = jnp.where(jnp.bitwise_and(target, 3) == j, jnp.right_shift(target, 2), -1)
        row_of = jnp.where(target < 0, -1, row_of)

        @pl.loop(0, NL // 256)
        def _(b, j=j, row_of=row_of):
            at = (pl.ds(pl.multiple_of(b * 256, 256), 256), pl.ds(j * 256, 256))
            delta = dot(onehot(256, row_of - b * 256), values)
            tile[at] = (tile[at].astype(F32) + delta).astype(BF16)

    def half_product(h):
        locals_[2 + h].wait()
        for g, steps in enumerate(GROUPS):
            wait_group(hs.at[h], hr_r.at[h], g)
            for s in steps:
                zs = lax.rem(z - ORDER[s] + NZ, NZ)
                for xs in range(NX):
                    pair = [hr[h, xs * NK + kk, s].astype(F32) for kk in range(NK)]
                    at = pl.ds(pl.multiple_of((xs * NZ + zs) * 16, 16), 16)
                    halo[h, at, :] = jnp.concatenate(pair, axis=0).astype(BF16)
        for i in (2, 1, 3, 0):
            cc = lax.rem(c + i, NC)
            block = tile[pl.ds(pl.multiple_of(cc * 256, 256), 256), :]
            share = dot(block, halo[h]).astype(BF16)
            if i == 0:
                own[h] = share
            else:
                ps[h, i - 1] = share
                pltpu.make_async_remote_copy(
                    ps.at[h, i - 1], pr.at[h, i - 1], p_s.at[h], p_r.at[h],
                    device_id=(me, cc), device_id_type=MESH,
                ).start()

    half_product(0)
    half_product(1)

    preact = jnp.zeros((256, D), F32)
    for h in (0, 1):
        pltpu.make_async_copy(pr.at[h], pr.at[h], p_r.at[h]).wait()
        neighbours = own[h].astype(F32)
        for i in range(NC - 1):
            neighbours = neighbours + pr[h, i].astype(F32)
        at = pl.ds(h * HALF, HALF)
        wide = emb[:, at].astype(F32)
        self_sum = (neighbours + wide).astype(BF16)
        inter = (neighbours * wide).astype(BF16)
        preact = preact + dot(self_sum, ws[at, :]) + dot(inter, wi[at, :])
    layer = jnp.where(preact >= 0, preact, 0.2 * preact)
    out[...] = jnp.where(aff[0] > 0, layer, emb[...].astype(F32)).astype(BF16)

    for h in (0, 1):
        for g in range(len(GROUPS)):
            wait_group(hs.at[h], hs_s.at[h], g)
        pltpu.make_async_copy(ps.at[h], ps.at[h], p_s.at[h]).wait()
    for g in range(len(GROUPS)):
        wait_group(us, us_s, g)
    some = ts.at[pl.ds(0, NZ - 1)]
    pltpu.make_async_copy(some, some, ts_s).wait()


def per_device(
    embeddings, adjacency, upd_vals, upd_dest, upd_target, upd_count,
    send_row, send_dest, affected, w_self, w_inter,
):
    v = pl.BlockSpec(memory_space=pltpu.VMEM)
    a = pl.BlockSpec(memory_space=pltpu.HBM)
    vm = pltpu.VMEM
    dma = pltpu.SemaphoreType.DMA
    n = len(GROUPS)
    u, r = upd_dest.shape[0], send_dest.shape[0]
    ints = jnp.concatenate(
        [
            upd_dest.reshape(1, u), upd_target.reshape(1, u), send_row.reshape(1, r),
            send_dest.reshape(1, r),
        ],
        axis=1,
    )
    return pl.pallas_call(
        kernel,
        out_shape=jax.ShapeDtypeStruct((D, D), BF16),
        in_specs=[a] * 8,
        out_specs=v,
        scratch_shapes=[
            pltpu.SMEM((1,), I32), pltpu.SMEM((1,), I32), vm((1, 1536), I32), vm((D, D), BF16), vm((u, D), BF16), vm((D, D), BF16), vm((D, D), BF16),
            dma((7,)),
            vm((NL, NL), BF16),
            vm((NZ, NQ, 8, 128), BF16),
            vm((NQ, NZ, 8, 128), BF16),
            vm((NZ, 1, 128), I32),
            vm((NZ, 1, 128), I32),
            vm((NQ, NZ, 1, 128), I32),
            vm((2, NZ, NQ, CAPR, HALF), BF16),
            vm((2, NQ, NZ, CAPR, HALF), BF16),
            vm((2, OWNERS * CAPR, HALF), BF16),
            vm((128, 128), I32),
            vm((2, NC - 1, 256, HALF), BF16),
            vm((2, NC - 1, 256, HALF), BF16),
            vm((2, 256, HALF), BF16),
            dma, dma((n,)), dma, dma((2, n)), dma((NZ,)), dma((4,)),
            dma, dma((n,)), dma, dma((2, n)), dma, dma((2,)), dma((2,)),
        ],
        compiler_params=pltpu.CompilerParams(
            collective_id=0, has_side_effects=True, vmem_limit_bytes=3440 * 2**14
        ),
    )(upd_count, affected, ints, embeddings, adjacency, upd_vals, w_self, w_inter)


def solution(mesh):
    rows = P(("owner", "col"))
    wide = P(("owner", "col"), None)
    return jax.shard_map(
        per_device,
        mesh=mesh,
        in_specs=(wide, P("owner", "col"), wide, wide, rows, rows, rows, wide, rows, P(), P()),
        out_specs=wide,
        check_vma=False,
    )
```

```python
import functools

import jax
import jax.numpy as jnp
from jax import lax
from jax.experimental import pallas as pl
from jax.experimental.pallas import tpu as pltpu
from jax.sharding import PartitionSpec as P

MESH = pl.DeviceIdType.MESH
BF16, F32, I32 = jnp.bfloat16, jnp.float32, jnp.int32
NX, NZ, NK, NC = 4, 16, 2, 4
NQ = NX * NK
OWNERS = NX * NZ * NK
CAPR, CAPU = 8, 4
D = 256
NL = 1024
ORDER = [8] + [s * d for d in range(7, 0, -1) for s in (1, -1)] + [0]
GROUPS = [range(0, 4), range(4, 8), range(8, 12), range(12, 15), range(15, 16)]
PIECES = 2
PIECE = 256 // PIECES
HALF = D // 2

def owner_of(x, z, k):
    return (x * NZ + z) * NK + k


def iota(shape, dim):
    return lax.broadcasted_iota(I32, shape, dim)


def dot(a, b):
    return jnp.dot(a, b, preferred_element_type=F32)


def dot_t(a, b):
    return lax.dot_general(a, b, (((1,), (1,)), ((), ())), preferred_element_type=F32)


def ranks(dest, live):
    n = dest.shape[1]
    hot = iota((OWNERS, n), 0) == dest
    if live is not None:
        hot = jnp.logical_and(hot, live)
    hot = jnp.where(hot, 1.0, 0.0)
    before = jnp.where(iota((n, n), 0) < iota((n, n), 1), 1.0, 0.0).astype(BF16)
    running = dot(hot.astype(BF16), before)
    return jnp.sum(running * hot, axis=0, keepdims=True).astype(I32)


def split_owner(dest):
    z = jnp.bitwise_and(jnp.right_shift(dest, 1), NZ - 1)
    q = jnp.right_shift(dest, 5) * NK + jnp.bitwise_and(dest, 1)
    return z, q


def onehot(rows, lane_index):
    return jnp.where(iota((rows, lane_index.shape[1]), 0) == lane_index, 1.0, 0.0).astype(BF16)


def kernel(
    cnt_h, aff_h, ints_h, emb_h, adj, uval_h, ws_h, wi_h,
    out,
    cnt, aff, ints, emb, uval, ws, wi, in_sem,
    tile, us, ur, ts, tz, tr, hs, hr, halo, tmat, ps, pr, own,
    adj_sem, us_s, ts_s, hs_s, tz_r, loc,
    tr_s, ur_r, tr_r, hr_r, own_t_s, p_s, p_r,
):
    me, c = lax.axis_index("owner"), lax.axis_index("col")
    x, z, k = me // (NZ * NK), lax.rem(me // NK, NZ), lax.rem(me, NK)
    q = x * NK + k

    def zdev(step, sign):
        return (owner_of(x, lax.rem(z + sign * ORDER[step] + NZ, NZ), k), c)

    def qdev(i):
        return lax.rem(x + i // NK, NX), lax.rem(k + i % NK, NK)

    adj_copy = pltpu.make_async_copy(adj, tile, adj_sem)
    inputs = [
        pltpu.make_async_copy(src, dst, in_sem.at[i])
        for i, (src, dst) in enumerate(
            (
                (ints_h, ints), (uval_h, uval), (cnt_h, cnt), (aff_h, aff), (emb_h, emb), (ws_h, ws), (wi_h, wi),
            )
        )
    ]
    for copy in inputs:
        copy.start()
    adj_copy.start()

    barrier = pltpu.get_barrier_semaphore()
    greeted = []
    for s in range(NZ):
        for i in range(NQ):
            if s < NZ - 1 or i:
                xx, kk = qdev(i)
                greeted.append((owner_of(xx, lax.rem(z + ORDER[s] + NZ, NZ), kk), c))
    greeted += [(me, lax.rem(c + i, NC)) for i in range(1, NC)]
    for dev in greeted:
        pl.semaphore_signal(barrier, inc=1, device_id=dev, device_id_type=MESH)

    for copy in inputs[:3]:
        copy.wait()
    udst, utgt = ints[:, 0:256], ints[:, 256:512]
    srow, sdst = ints[:, 512:1024], ints[:, 1024:1536]
    dest = udst
    live = iota(dest.shape, 1) < cnt[0]
    rank = ranks(dest, live)
    zz, qq = split_owner(dest)
    slot = jnp.where(live, zz * (NQ * 8) + qq * 8 + rank, -8)
    slot2 = jnp.concatenate([slot, slot + CAPU], axis=1)
    vals = uval[...]
    stacked = jnp.concatenate([vals[:, :128], vals[:, 128:]], axis=0)
    us[...] = dot(onehot(NZ * NQ * 8, slot2), stacked).astype(BF16).reshape(NZ, NQ, 8, 128)
    tgt = utgt + 1
    row_z = jnp.where(jnp.logical_and(iota((NZ, dest.shape[1]), 0) == zz, live), 1.0, 0.0)
    lane_q = onehot(128, qq * CAPU + rank)
    hi = (row_z * jnp.right_shift(tgt, 6).astype(F32)).astype(BF16)
    lo = (row_z * jnp.bitwise_and(tgt, 63).astype(F32)).astype(BF16)
    sent_targets = (dot_t(hi, lane_q) * 64.0 + dot_t(lo, lane_q)).astype(I32)
    for i in range(NZ):
        ts[i] = sent_targets[i : i + 1]

    pl.semaphore_wait(barrier, len(greeted))

    def zcopy(src, dst, send, recv, step):
        dev = zdev(step, 1)
        return pltpu.make_async_remote_copy(
            src.at[lax.rem(z + ORDER[step] + NZ, NZ)], dst.at[step], send, recv.at[step],
            device_id=dev, device_id_type=MESH,
        )

    def direct(src, dst, send, recv):
        for i in (5, 3, 7, 1, 4, 2, 6, 0):
            for s in range(NZ):
                zz = lax.rem(z + ORDER[s] + NZ, NZ)
                g = [g for g, steps in enumerate(GROUPS) if s in steps][0]
                if s < NZ - 1 or i:
                    xx, kk = qdev(i)
                    pltpu.make_async_remote_copy(
                        src.at[zz, xx * NK + kk], dst.at[q, s], send.at[g], recv.at[g],
                        device_id=(owner_of(xx, zz, kk), c), device_id_type=MESH,
                    ).start()

    def wait_group(src, sem, g):
        some = src.at[pl.ds(0, len(GROUPS[g]))]
        if g == len(GROUPS) - 1:
            some = src.at[0, pl.ds(0, NQ - 1)]
        pltpu.make_async_copy(some, some, sem.at[g]).wait()

    tcopies = [zcopy(ts, tz, ts_s, tz_r, s) for s in range(NZ - 1)]
    for s in range(NZ - 1):
        tcopies[s].start()
    direct(us, ur, us_s, ur_r)
    locals_ = [
        pltpu.make_async_copy(us.at[z, q], ur.at[q, NZ - 1], loc.at[0]),
        pltpu.make_async_copy(ts.at[z], tz.at[NZ - 1], loc.at[1]),
    ]
    for copy in locals_:
        copy.start()

    for copy in inputs[3:]:
        copy.wait()
    dest = sdst
    rank = ranks(dest, None)
    zz, qq = split_owner(dest)
    place = onehot(OWNERS * CAPR, zz * (NQ * CAPR) + qq * CAPR + rank)
    pick = dot_t(place, onehot(D, srow)).astype(BF16)
    rows = dot(pick, emb[...]).astype(BF16)
    for h in (0, 1):
        hs[h] = rows[:, h * HALF : (h + 1) * HALF].reshape(NZ, NQ, CAPR, HALF)
    direct(hs.at[0], hr.at[0], hs_s.at[0], hr_r.at[0])
    for h in (0, 1):
        locals_.append(pltpu.make_async_copy(hs.at[h, z, q], hr.at[h, q, NZ - 1], loc.at[2 + h]))
        locals_[2 + h].start()

    for s in range(NZ - 1):
        tcopies[s].wait_recv()
    locals_[1].wait()
    for i in range(1, NQ):
        xx, kk = qdev(i)
        pltpu.make_async_remote_copy(
            tz, tr.at[q], tr_s, tr_r, device_id=(owner_of(xx, z, kk), c), device_id_type=MESH
        ).start()
    own_t = pltpu.make_async_copy(tz, tr.at[q], own_t_s)
    own_t.start()
    direct(hs.at[1], hr.at[1], hs_s.at[1], hr_r.at[1])
    own_t.wait()
    some = tr.at[pl.ds(0, NQ - 1)]
    pltpu.make_async_copy(some, some, tr_r).wait()
    pltpu.make_async_copy(some, some, tr_s).wait()
    locals_[0].wait()
    for g in range(len(GROUPS)):
        wait_group(us, ur_r, g)

    for i in range(OWNERS):
        tmat[i : i + 1] = tr[i // NZ, i % NZ]
    got = tmat[...].astype(F32)
    eye = iota((128, 128), 0) == iota((128, 128), 1)
    lanes = []
    for s in range(CAPU):
        column = jnp.sum(jnp.where(iota((128, 128), 1) == q * CAPU + s, got, 0.0), axis=1, keepdims=True)
        lanes.append(jnp.sum(jnp.where(eye, column, 0.0), axis=0, keepdims=True))
    target = jnp.concatenate(lanes, axis=1).astype(I32) - 1
    packed = ur[...].reshape(OWNERS * 8, 128)
    u_row = iota((OWNERS * CAPU, OWNERS * 8), 0)
    u_from = jnp.bitwise_and(u_row, 127) * 8 + jnp.right_shift(u_row, 7)
    m_col = iota((OWNERS * CAPU, OWNERS * 8), 1)
    halves = [
        dot(jnp.where(m_col == u_from + h * CAPU, 1.0, 0.0).astype(BF16), packed) for h in (0, 1)
    ]
    values = jnp.concatenate(halves, axis=1).astype(BF16)

    adj_copy.wait()
    for j in range(4):
        row_of = jnp.where(jnp.bitwise_and(target, 3) == j, jnp.right_shift(target, 2), -1)
        row_of = jnp.where(target < 0, -1, row_of)

        @pl.loop(0, NL // 256)
        def _(b, j=j, row_of=row_of):
            at = (pl.ds(pl.multiple_of(b * 256, 256), 256), pl.ds(j * 256, 256))
            delta = dot(onehot(256, row_of - b * 256), values)
            tile[at] = (tile[at].astype(F32) + delta).astype(BF16)

    def half_product(h):
        locals_[2 + h].wait()
        for g, steps in enumerate(GROUPS):
            wait_group(hs.at[h], hr_r.at[h], g)
            for s in steps:
                zs = lax.rem(z - ORDER[s] + NZ, NZ)
                for xs in range(NX):
                    pair = [hr[h, xs * NK + kk, s].astype(F32) for kk in range(NK)]
                    at = pl.ds(pl.multiple_of((xs * NZ + zs) * 16, 16), 16)
                    halo[h, at, :] = jnp.concatenate(pair, axis=0).astype(BF16)
        for b in range(PIECES):
            for i in (2, 1, 3, 0):
                cc = lax.rem(c + i, NC)
                at = pl.ds(pl.multiple_of(cc * 256 + b * PIECE, PIECE), PIECE)
                share = dot(tile[at, :], halo[h]).astype(BF16)
                if i == 0:
                    own[h, b] = share
                else:
                    ps[h, b, i - 1] = share
                    pltpu.make_async_remote_copy(
                        ps.at[h, b, i - 1], pr.at[h, b, i - 1], p_s.at[h, b], p_r.at[h, b],
                        device_id=(me, cc), device_id_type=MESH,
                    ).start()

    half_product(0)
    half_product(1)

    for b in range(PIECES):
        rows = pl.ds(b * PIECE, PIECE)
        preact = jnp.zeros((PIECE, D), F32)
        for h in (0, 1):
            pltpu.make_async_copy(pr.at[h, b], pr.at[h, b], p_r.at[h, b]).wait()
            neighbours = own[h, b].astype(F32)
            for i in range(NC - 1):
                neighbours = neighbours + pr[h, b, i].astype(F32)
            at = pl.ds(h * HALF, HALF)
            wide = emb[rows, at].astype(F32)
            self_sum = (neighbours + wide).astype(BF16)
            inter = (neighbours * wide).astype(BF16)
            preact = preact + dot(self_sum, ws[at, :]) + dot(inter, wi[at, :])
        layer = jnp.where(preact >= 0, preact, 0.2 * preact)
        out[rows, :] = jnp.where(aff[0] > 0, layer, emb[rows, :].astype(F32)).astype(BF16)

    for h in (0, 1):
        for g in range(len(GROUPS)):
            wait_group(hs.at[h], hs_s.at[h], g)
        for b in range(PIECES):
            pltpu.make_async_copy(ps.at[h, b], ps.at[h, b], p_s.at[h, b]).wait()
    for g in range(len(GROUPS)):
        wait_group(us, us_s, g)
    some = ts.at[pl.ds(0, NZ - 1)]
    pltpu.make_async_copy(some, some, ts_s).wait()


def per_device(
    embeddings, adjacency, upd_vals, upd_dest, upd_target, upd_count,
    send_row, send_dest, affected, w_self, w_inter,
):
    v = pl.BlockSpec(memory_space=pltpu.VMEM)
    a = pl.BlockSpec(memory_space=pltpu.HBM)
    vm = pltpu.VMEM
    dma = pltpu.SemaphoreType.DMA
    n = len(GROUPS)
    u, r = upd_dest.shape[0], send_dest.shape[0]
    ints = jnp.concatenate(
        [
            upd_dest.reshape(1, u), upd_target.reshape(1, u), send_row.reshape(1, r),
            send_dest.reshape(1, r),
        ],
        axis=1,
    )
    return pl.pallas_call(
        kernel,
        out_shape=jax.ShapeDtypeStruct((D, D), BF16),
        in_specs=[a] * 8,
        out_specs=v,
        scratch_shapes=[
            pltpu.SMEM((1,), I32), pltpu.SMEM((1,), I32), vm((1, 1536), I32), vm((D, D), BF16), vm((u, D), BF16), vm((D, D), BF16), vm((D, D), BF16),
            dma((7,)),
            vm((NL, NL), BF16),
            vm((NZ, NQ, 8, 128), BF16),
            vm((NQ, NZ, 8, 128), BF16),
            vm((NZ, 1, 128), I32),
            vm((NZ, 1, 128), I32),
            vm((NQ, NZ, 1, 128), I32),
            vm((2, NZ, NQ, CAPR, HALF), BF16),
            vm((2, NQ, NZ, CAPR, HALF), BF16),
            vm((2, OWNERS * CAPR, HALF), BF16),
            vm((128, 128), I32),
            vm((2, PIECES, NC - 1, PIECE, HALF), BF16),
            vm((2, PIECES, NC - 1, PIECE, HALF), BF16),
            vm((2, PIECES, PIECE, HALF), BF16),
            dma, dma((n,)), dma, dma((2, n)), dma((NZ,)), dma((4,)),
            dma, dma((n,)), dma, dma((2, n)), dma, dma((2, PIECES)), dma((2, PIECES)),
        ],
        compiler_params=pltpu.CompilerParams(
            collective_id=0, has_side_effects=True, vmem_limit_bytes=3440 * 2**14
        ),
    )(upd_count, affected, ints, embeddings, adjacency, upd_vals, w_self, w_inter)


def solution(mesh):
    rows = P(("owner", "col"))
    wide = P(("owner", "col"), None)
    return jax.shard_map(
        per_device,
        mesh=mesh,
        in_specs=(wide, P("owner", "col"), wide, wide, rows, rows, rows, wide, rows, P(), P()),
        out_specs=wide,
        check_vma=False,
    )
```
